32 devices in a mesh: elem: 32 (over z, y, x, core).
Axes of the slice: x: 2, y: 2, z: 4, core: 2. Of those that a mesh axis runs over, the one named last changes fastest.
Arguments:
- tracer: float32 [256, 8, 640], P('elem'), may hold values from 0 to 1
- old_mass: float32 [256, 128], P('elem'), may hold values from 0.3 to 3
- new_mass: float32 [256, 128], P('elem'), may hold values from 0.3 to 3
- dep_owner: int32 [256, 128, 1], P('elem'), may hold values from 0 to 31, as said below
- dep_local: int32 [256, 128], P('elem'), may hold values from 0 to 7
- dep_coord: float32 [2, 256, 128], P(None, 'elem'), may hold values from -1 to 1
Outputs:
- new_tracer: float32 [256, 8, 640], P('elem')
The draws below stay inside these ranges and needn't reach their ends.
Inputs may be any that keep to these rules, and one draw needn't show every extreme that they name: `dep_owner`: the rows of one device name their own device or one of at most five other devices; no other device is named more than 32 times among them, and one other device is named exactly 32 times.
All inputs are finite; a program needn't handle non-finite values.
Results may differ from the reference program's by a relative error of at most 0.0003.
Values sent between devices are 32-bit elements; how exact they have to be, the bound alone decides.
A program may use at most 64 MiB of HBM per device.

```python
import math
import jax
import jax.numpy as jnp
from jax import lax

E_DEV = 8
LEV = 8
NP2 = 16
Q = 40
ELEMS = 256
N_ELEM = 32


def draw_dep_owner(key, part):
    rows = E_DEV * LEV * NP2
    bound = rows // 32
    keys = jax.random.split(jax.random.fold_in(key, 7031), N_ELEM)
    devices = jnp.arange(N_ELEM, dtype=jnp.int32)

    def one_device(dev_key, device):
        key_count, key_pick, key_perm, key_peer = jax.random.split(dev_key, 4)
        shuffled = jax.random.permutation(key_peer, N_ELEM - 1).astype(jnp.int32) + 1
        offsets = shuffled[:5]
        counts = jax.random.randint(key_count, (5,), max(1, bound // 4), bound + 1, dtype=jnp.int32)
        pick = jax.random.randint(key_pick, (), 0, 5, dtype=jnp.int32)
        counts = jnp.where(jnp.arange(5, dtype=jnp.int32) == pick, bound, counts)
        limits = jnp.cumsum(counts)
        position = jnp.arange(rows, dtype=jnp.int32)
        which = jnp.sum((position[:, None] >= limits[None, :]).astype(jnp.int32), axis=1)
        neighbour = (device + offsets[jnp.minimum(which, 4)]) % N_ELEM
        owners = jnp.where(which < 5, neighbour, device).astype(jnp.int32)
        order = jax.random.permutation(key_perm, rows)
        return owners[order]
    owners = jax.vmap(one_device)(keys, devices)
    return owners.reshape(N_ELEM * E_DEV, LEV * NP2, 1).astype(jnp.int32)


def plant(drawn, rng, least, top_value):
    longest = drawn.shape.index(max(drawn.shape))
    spots = []
    for shift in (0, 1):
        where = [jax.random.randint(jax.random.fold_in(rng, axis), (), 0, length) for axis, length in enumerate(drawn.shape)]
        where[longest] = (where[longest] + shift) % drawn.shape[longest]
        spots.append(tuple(where))
    return drawn.at[spots[0]].set(least).at[spots[1]].set(top_value)


def shard_levels(rng, shape, cuts, least, top_value):
    gain, own = 1.0, jax.random.fold_in(rng, 6)
    for dim, parts in cuts:
        steps = jnp.exp(jax.random.uniform(jax.random.fold_in(own, dim), (parts,), jnp.float32, least / len(cuts), top_value / len(cuts)))
        gain = gain * jnp.repeat(steps, shape[dim] // parts).reshape([-1 if axis == dim else 1 for axis in range(len(shape))])
    return gain


def setup_inputs(seed: int = 0) -> dict:
    key_list = jax.random.split(jax.random.key(seed), 7)
    return {
        "tracer": jnp.clip(1.0 * jax.random.uniform(key_list[0], (ELEMS, LEV, NP2 * Q), jnp.float32) ** shard_levels(key_list[0], (ELEMS, LEV, NP2 * Q), ((0, 32),), -0.2, 0.2), 0.0, 1.0),
        "old_mass": jnp.clip(jnp.exp(math.log(3.0) - 2.3025851 * jax.random.uniform(key_list[1], (ELEMS, LEV * NP2), jnp.float32) ** shard_levels(key_list[1], (ELEMS, LEV * NP2), ((0, 32),), -0.2, 0.2)), 0.3, 3.0),
        "new_mass": jnp.clip(jnp.exp(math.log(3.0) - 2.3025851 * jax.random.uniform(key_list[2], (ELEMS, LEV * NP2), jnp.float32) ** shard_levels(key_list[2], (ELEMS, LEV * NP2), ((0, 32),), -0.2, 0.2)), 0.3, 3.0),
        "dep_owner": draw_dep_owner(jax.random.fold_in(key_list[6], 71), 0),
        "dep_local": plant(jax.random.randint(key_list[4], (ELEMS, LEV * NP2), 0, E_DEV), jax.random.fold_in(key_list[4], 1), 0, E_DEV - 1).astype(jnp.int32),
        "dep_coord": jnp.clip(jax.random.uniform(key_list[5], (2, ELEMS, LEV * NP2), jnp.float32, -1.0, 1.0) * shard_levels(key_list[5], (2, ELEMS, LEV * NP2), ((1, 32),), -0.4, 0.0), -1.0, 1.0),
    }


GLL_NODES = (-1.0, -0.4472135954999579, 0.4472135954999579, 1.0)


def one_axis(coord):
    columns = []
    for node_own in range(4):
        factor = jnp.ones_like(coord)
        for node_other in range(4):
            if node_other != node_own:
                factor = factor * (coord - GLL_NODES[node_other]) / (GLL_NODES[node_own] - GLL_NODES[node_other])
        columns.append(factor)
    return jnp.stack(columns, axis=-1)


def lagrange_weights(coord_a, coord_b):
    weights_a = one_axis(coord_a)
    weights_b = one_axis(coord_b)
    return (weights_a[..., :, None] * weights_b[..., None, :]).reshape(coord_a.shape + (16,))


def fixer_terms(interp, lowest, highest, mass_new):
    clipped = jnp.clip(interp, lowest, highest)
    margin = 0.01 + 0.05 * (highest - lowest)
    upper = highest + margin - clipped
    lower = clipped - lowest + margin
    sums = (jnp.sum(mass_new * clipped, axis=(0, 2)), jnp.sum(mass_new * upper, axis=(0, 2)), jnp.sum(mass_new * lower, axis=(0, 2)))
    return clipped, upper, lower, sums


def apply_fix(clipped, upper, lower, source_total, clip_total, up_total, down_total):
    deficit = (source_total - clip_total)[:, None, :]
    return clipped + jnp.maximum(deficit, 0.0) / up_total[:, None, :] * upper + jnp.minimum(deficit, 0.0) / down_total[:, None, :] * lower


def reference(tracer, old_mass, new_mass, dep_owner, dep_local, dep_coord):
    elems, levels, width = tracer.shape
    tracers = width // NP2
    table = tracer.reshape(elems * levels, width)
    level_index = jnp.arange(levels * NP2, dtype=jnp.int32) // NP2
    groups = elems // E_DEV

    def block_eval(inputs):
        owners, local_ids, coord_a, coord_b = inputs
        row_ids = ((owners * E_DEV + local_ids) * levels + level_index[None, :]).astype(jnp.int32)
        source = table[row_ids].reshape(row_ids.shape + (NP2, tracers))
        weights = lagrange_weights(coord_a, coord_b)
        interp = jnp.einsum("elk,elkq->elq", weights, source, precision=lax.Precision.HIGHEST)
        return interp, jnp.min(source, axis=2), jnp.max(source, axis=2)

    interp, lowest, highest = lax.map(block_eval, (dep_owner[..., 0].reshape(groups, E_DEV, -1), dep_local.reshape(groups, E_DEV, -1), dep_coord[0].reshape(groups, E_DEV, -1), dep_coord[1].reshape(groups, E_DEV, -1)))
    shape4 = (elems, levels, NP2, tracers)
    interp = interp.reshape(shape4)
    lowest = lowest.reshape(shape4)
    highest = highest.reshape(shape4)
    mass_new = new_mass.reshape(elems, levels, NP2, 1)
    source_total = jnp.sum(old_mass.reshape(elems, levels, NP2, 1) * tracer.reshape(shape4), axis=(0, 2))
    clipped, upper, lower, sums = fixer_terms(interp, lowest, highest, mass_new)
    result = apply_fix(clipped, upper, lower, source_total, sums[0], sums[1], sums[2])
    return result.reshape(elems, levels, width)
```

```python
import functools

import jax
import jax.numpy as jnp
from jax import lax
from jax.experimental import pallas as pl
from jax.experimental.pallas import tpu as pltpu
from jax.sharding import PartitionSpec as P

GLL_NODES = (-1.0, -0.4472135954999579, 0.4472135954999579, 1.0)
NODES = 16
MESH = pl.DeviceIdType.MESH
F32 = jnp.float32
BF16 = jnp.bfloat16
HIGHEST = lax.Precision.HIGHEST


def one_axis(coord):
    away = [coord - node for node in GLL_NODES]
    columns = []
    for own in range(4):
        factor, scale = None, 1.0
        for other in range(4):
            if other != own:
                factor = away[other] if factor is None else factor * away[other]
                scale *= GLL_NODES[own] - GLL_NODES[other]
        columns.append(factor * (1.0 / scale))
    return columns


def split3(x):
    high = x.astype(BF16).astype(F32)
    rest = x - high
    middle = rest.astype(BF16).astype(F32)
    return high, middle, rest - middle


def iota(shape, axis):
    return lax.broadcasted_iota(jnp.int32, shape, axis)


def dot_nt(a, b, precision=None):
    return lax.dot_general(
        a, b, (((1,), (1,)), ((), ())), precision=precision, preferred_element_type=F32
    )


def dot_tn(a, b, precision=None):
    return lax.dot_general(
        a, b, (((0,), (0,)), ((), ())), precision=precision, preferred_element_type=F32
    )


def kernel(
    devices, cap,
    tracer, old_mass, new_mass, owner, local, coord, out,
    table, home_c, home_u, home_l, far_c, far_u, far_l, spread, la_home, la_far, fields,
    req_out, req_in, sum_out, sum_in, ans_out, ans_in, turned,
    req_send, req_recv, sum_send, sum_recv, ans_send, ans_recv,
):
    elems, levels, width = tracer.shape
    tracers = width // NODES
    points = levels * NODES
    cells = elems * levels
    group = points // cap
    blocks = devices // group
    me = lax.axis_index("elem")

    def peer(step):
        return lax.rem(me + step, devices)

    barrier = pltpu.get_barrier_semaphore()

    @pl.loop(1, devices)
    def _(step):
        pl.semaphore_signal(barrier, inc=1, device_id=(peer(step),), device_id_type=MESH)

    own = owner[...]
    away_ids = iota((devices, points), 0)
    away_ids = jnp.where(away_ids == me, -1, away_ids)
    hot = [(own[e : e + 1, :] == away_ids).astype(F32) for e in range(elems)]
    row, column = iota((points, 2 * points), 0), iota((points, 2 * points), 1)
    ladder = ((row <= column) | (column >= points)).astype(BF16)
    counted = jnp.dot(jnp.concatenate(hot, axis=0).astype(BF16), ladder, preferred_element_type=F32)
    before = jnp.zeros((devices, points), F32)
    base = (away_ids * cap).astype(F32)
    ranks, slots = [], []
    for e in range(elems):
        part = counted[e * devices : (e + 1) * devices]
        rank = jnp.sum(hot[e] * (part[:, :points] + before), axis=0, keepdims=True) - 1.0
        ranks.append(rank)
        slots.append(jnp.sum(hot[e] * base, axis=0, keepdims=True) + rank)
        before = before + part[:, points:]

    level_of = lax.div(iota((elems, points), 1), NODES)
    cell_home = (local[...] * levels + level_of).astype(F32)
    payload = [split3(x) for x in (cell_home, coord[0], coord[1], new_mass[...])]
    place = iota((cap, points), 0).astype(F32)
    chosen = []
    for term in range(3):
        lanes = []
        for e in range(elems):
            mine = place == ranks[e]
            lanes.append(
                jnp.concatenate(
                    [jnp.where(mine, f[term][e : e + 1, :], 0.0) for f in payload], axis=0
                ).astype(BF16)
            )
        chosen.append(jnp.concatenate(lanes, axis=1))
    hots = jnp.concatenate([h.astype(BF16) for h in hot], axis=1)
    asked = dot_nt(hots, chosen[0]) + dot_nt(hots, chosen[1]) + dot_nt(hots, chosen[2])
    req_out[...] = asked.reshape(devices, 1, points)
    req_in[pl.ds(me, 1)] = jnp.zeros((1, 1, points), F32)

    pl.semaphore_wait(barrier, devices - 1)

    def request(to, source):
        return pltpu.make_async_remote_copy(
            src_ref=req_out.at[to], dst_ref=req_in.at[source],
            send_sem=req_send.at[to], recv_sem=req_recv.at[source],
            device_id=(to,), device_id_type=MESH,
        )

    @pl.loop(1, devices)
    def _(step):
        request(peer(step), me).start()

    flat = tracer[...].reshape(cells, width)
    table[...] = jnp.concatenate(split3(flat), axis=0).T.astype(BF16)

    point = iota((levels, points), 1)
    at_level = lax.div(point, NODES) == iota((levels, points), 0)
    masses = jnp.concatenate(
        [jnp.where(at_level, old_mass[e : e + 1, :], 0.0) for e in range(elems)], axis=0
    )
    widen = (
        lax.rem(iota((points, width), 0), NODES) == lax.div(iota((points, width), 1), tracers)
    ).astype(BF16)
    wide = jnp.zeros((cells, width), F32)
    for term in split3(masses):
        wide = wide + jnp.dot(term.astype(BF16), widen, preferred_element_type=F32)
    held = wide * flat
    by_node = held[:levels]
    for e in range(1, elems):
        by_node = by_node + held[e * levels : (e + 1) * levels]
    narrow = (lax.rem(iota((width, points), 0), tracers) == iota((width, points), 1)).astype(F32)
    source = jnp.dot(by_node, narrow, precision=HIGHEST, preferred_element_type=F32)

    cell_ids = lax.rem(iota((3 * cells, points), 0), cells).astype(F32)

    def evaluate(cell, wa, wb):
        chosen = (cell_ids == cell).astype(BF16)
        values = jnp.dot(table[...], chosen, preferred_element_type=F32)
        interp = lowest = highest = None
        for k in range(NODES):
            value = values[k * tracers : (k + 1) * tracers]
            term = (wa[k // 4] * wb[k % 4]) * value
            interp = term if k == 0 else interp + term
            lowest = value if k == 0 else jnp.minimum(lowest, value)
            highest = value if k == 0 else jnp.maximum(highest, value)
        clipped = jnp.minimum(jnp.maximum(interp, lowest), highest)
        margin = 0.01 + 0.05 * (highest - lowest)
        return clipped, highest + margin - clipped, clipped - lowest + margin

    def mass_sums(weights, clipped, upper, lower):
        rest = jnp.zeros((points - 3 * tracers, points), F32)
        terms = jnp.concatenate([-clipped, upper, lower, rest], axis=0)
        return dot_nt(weights, terms, HIGHEST)

    for i, value in enumerate(one_axis(coord[0]) + one_axis(coord[1])):
        la_home[i] = value.reshape(elems, 1, points)
    fields[pl.ds(0, elems)] = cell_home.reshape(elems, 1, points)
    fields[pl.ds(elems, elems)] = jnp.where(own == me, new_mass[...], 0.0).reshape(
        elems, 1, points
    )

    def home_block(e, sums):
        results = evaluate(
            fields[e], [la_home[i, e] for i in range(4)], [la_home[4 + i, e] for i in range(4)]
        )
        home_c[e], home_u[e], home_l[e] = results
        weights = jnp.where(at_level, fields[elems + e], 0.0)
        return sums + mass_sums(weights, *results)

    sums = lax.fori_loop(0, elems, home_block, source)

    slot_ids = iota((devices * cap, points), 0).astype(F32)
    for e in range(elems):
        spread[:, e * points : (e + 1) * points] = (slot_ids == slots[e]).astype(BF16)

    @pl.loop(1, devices)
    def _(step):
        request(peer(step), peer(step)).wait_recv()

    got = req_in[...].reshape(devices, points)
    r, c = iota((devices, points), 0), lax.div(iota((devices, points), 1), cap)
    bit = 1
    while bit < group:
        down = pltpu.roll(pltpu.roll(got, bit, 0), points - cap * bit, 1)
        up = pltpu.roll(pltpu.roll(got, devices - bit, 0), cap * bit, 1)
        row_bit, lane_bit = (r & bit) != 0, (c & bit) != 0
        got = jnp.where(row_bit == lane_bit, got, jnp.where(row_bit, down, up))
        bit *= 2
    la_far[4] = got.reshape(devices, 1, points)
    for i, value in enumerate(one_axis(got)):
        la_far[i] = value.reshape(devices, 1, points)

    level_ids = iota((levels, points), 0).astype(F32)

    def slot_level(b):
        cell = la_far[4, group * b]
        return cell, level_ids == cell - levels * jnp.floor((cell + 0.5) / levels)

    def far_block(b, sums):
        first = group * b
        cell, here = slot_level(b)
        results = evaluate(
            cell,
            [la_far[i, first + 1] for i in range(4)],
            [la_far[i, first + 2] for i in range(4)],
        )
        far_c[b], far_u[b], far_l[b] = results
        return sums + mass_sums(jnp.where(here, la_far[4, first + 3], 0.0), *results)

    sums = lax.fori_loop(0, blocks, far_block, sums)

    sum_out[...] = sums
    sum_in[pl.ds(me, 1)] = sums.reshape(1, levels, points)

    def share(to, source):
        return pltpu.make_async_remote_copy(
            src_ref=sum_out, dst_ref=sum_in.at[source],
            send_sem=sum_send.at[to], recv_sem=sum_recv.at[source],
            device_id=(to,), device_id_type=MESH,
        )

    @pl.loop(1, devices)
    def _(step):
        share(peer(step), me).start()

    @pl.loop(1, devices)
    def _(step):
        share(peer(step), peer(step)).wait_recv()

    total = jnp.sum(sum_in[...], axis=0)
    lane = iota((levels, points), 1)
    up_total = pltpu.roll(total, points - tracers, 1)
    down_total = pltpu.roll(total, points - 2 * tracers, 1)
    inside = lane < tracers
    plus = jnp.where(inside, jnp.maximum(total, 0.0) / jnp.where(inside, up_total, 1.0), 0.0)
    minus = jnp.where(inside, jnp.minimum(total, 0.0) / jnp.where(inside, down_total, 1.0), 0.0)
    factors = plus + pltpu.roll(minus, tracers, 1)

    def fix(here, clipped, upper, lower):
        by_lane = dot_tn(factors, here.astype(F32), HIGHEST)
        return clipped + by_lane[:tracers] * upper + by_lane[tracers : 2 * tracers] * lower

    def answer(to, source):
        return pltpu.make_async_remote_copy(
            src_ref=ans_out.at[to], dst_ref=ans_in.at[source],
            send_sem=ans_send.at[to], recv_sem=ans_recv.at[source],
            device_id=(to,), device_id_type=MESH,
        )

    lane_block = lax.div(iota((8, points), 1), cap)

    def swap_blocks(tiles):
        bit = 1
        while bit < group:
            moved = list(tiles)
            for t in range(group):
                if t & bit == 0:
                    odd = (lane_block & bit) != 0
                    a, b = tiles[t], tiles[t + bit]
                    moved[t] = jnp.where(odd, pltpu.roll(b, cap * bit, 1), a)
                    moved[t + bit] = jnp.where(odd, b, pltpu.roll(a, points - cap * bit, 1))
            tiles = moved
            bit *= 2
        return tiles

    my_place = lax.rem(me, group)

    def send_block(turn, carry):
        b = lax.rem(turn + lax.div(me, group), blocks)
        _, here = slot_level(b)
        fixed = fix(here, far_c[b], far_u[b], far_l[b])
        tiles = swap_blocks([fixed[8 * t : 8 * t + 8] for t in range(group)])
        last = fixed[8 * group :]
        for i in range(group):
            to = group * b + i
            ans_out[to, 0:8] = tiles[i]
            ans_out[to, 8:16] = pltpu.roll(last, lax.rem(my_place + group - i, group) * cap, 1)

            @pl.when(to != me)
            def _():
                answer(to, me).start()

        return carry

    lax.fori_loop(0, blocks, send_block, 0)

    def home_fix(e, carry):
        home_c[e] = fix(at_level, home_c[e], home_u[e], home_l[e])
        return carry

    lax.fori_loop(0, elems, home_fix, 0)
    ans_in[pl.ds(me, 1)] = jnp.zeros((1, 16, points), F32)

    @pl.loop(1, devices)
    def _(step):
        answer(peer(step), peer(step)).wait_recv()

    columns = []
    for b in range(blocks):
        tiles = swap_blocks([ans_in[group * b + i, 0:8] for i in range(group)])
        last = ans_in[group * b, 8:16]
        for i in range(1, group):
            last = jnp.where(lane_block == i, ans_in[group * b + i, 8:16], last)
        columns.append(jnp.concatenate(tiles + [last], axis=0))
    answers = jnp.concatenate(columns, axis=1)
    terms = jnp.concatenate(split3(answers), axis=0).astype(BF16)
    landed = jnp.dot(terms, spread[...], preferred_element_type=F32)
    landed = landed[:tracers] + landed[tracers : 2 * tracers] + landed[2 * tracers :]

    pad = jnp.zeros((points - tracers, points), F32)
    for e in range(elems):
        mixed = jnp.where(own[e : e + 1] == me, home_c[e], landed[:, e * points : (e + 1) * points])
        turned[e] = jnp.concatenate([mixed, pad], axis=0).T
        for k in range(NODES):
            out[e, :, k * tracers : (k + 1) * tracers] = turned[
                e, pl.ds(k, levels, stride=NODES), :
            ][:, :tracers]

    @pl.loop(1, devices)
    def _(step):
        to = peer(step)
        request(to, me).wait_send()
        share(to, me).wait_send()
        answer(to, me).wait_send()


def body(tracer, old_mass, new_mass, dep_owner, dep_local, dep_coord):
    devices = lax.axis_size("elem")
    elems, levels, width = tracer.shape
    tracers = width // NODES
    points = levels * NODES
    cap = elems * points // 32
    blocks = devices * cap // points
    cells = elems * levels
    vmem = pltpu.VMEM
    dma = pltpu.SemaphoreType.DMA
    return pl.pallas_call(
        functools.partial(kernel, devices, cap),
        out_shape=jax.ShapeDtypeStruct(tracer.shape, F32),
        in_specs=[pl.BlockSpec(memory_space=vmem)] * 6,
        out_specs=pl.BlockSpec(memory_space=vmem),
        scratch_shapes=[
            vmem((width, 3 * cells), BF16),
            *[vmem((elems, tracers, points), F32)] * 3,
            *[vmem((blocks, tracers, points), F32)] * 3,
            vmem((devices * cap, elems * points), BF16),
            vmem((8, elems, 1, points), F32),
            vmem((5, devices, 1, points), F32),
            vmem((2 * elems, 1, points), F32),
            vmem((devices, 1, points), F32),
            vmem((devices, 1, points), F32),
            vmem((levels, points), F32),
            vmem((devices, levels, points), F32),
            vmem((devices, 16, points), F32),
            vmem((devices, 16, points), F32),
            vmem((elems, points, points), F32),
            *[dma((devices,))] * 6,
        ],
        compiler_params=pltpu.CompilerParams(
            collective_id=0, has_side_effects=True, vmem_limit_bytes=48 * 1024 * 1024
        ),
    )(
        tracer, old_mass, new_mass,
        dep_owner.reshape(elems, points), dep_local, dep_coord,
    )


def solution(mesh):
    placed = (
        P("elem", None, None),
        P("elem", None),
        P("elem", None),
        P("elem", None, None),
        P("elem", None),
        P(None, "elem", None),
    )
    return jax.shard_map(
        body, mesh=mesh, in_specs=placed, out_specs=P("elem", None, None), check_vma=False
    )
```

```python
import functools

import jax
import jax.numpy as jnp
from jax import lax
from jax.experimental import pallas as pl
from jax.experimental.pallas import tpu as pltpu
from jax.sharding import PartitionSpec as P

GLL_NODES = (-1.0, -0.4472135954999579, 0.4472135954999579, 1.0)
NODES = 16
MESH = pl.DeviceIdType.MESH
F32 = jnp.float32
BF16 = jnp.bfloat16
HIGHEST = lax.Precision.HIGHEST


def one_axis(coord):
    away = [coord - node for node in GLL_NODES]
    columns = []
    for own in range(4):
        factor, scale = None, 1.0
        for other in range(4):
            if other != own:
                factor = away[other] if factor is None else factor * away[other]
                scale *= GLL_NODES[own] - GLL_NODES[other]
        columns.append(factor * (1.0 / scale))
    return columns


def split3(x):
    high = x.astype(BF16).astype(F32)
    rest = x - high
    middle = rest.astype(BF16).astype(F32)
    return high, middle, rest - middle


def iota(shape, axis):
    return lax.broadcasted_iota(jnp.int32, shape, axis)


def dot_nt(a, b, precision=None):
    return lax.dot_general(
        a, b, (((1,), (1,)), ((), ())), precision=precision, preferred_element_type=F32
    )


def dot_tn(a, b, precision=None):
    return lax.dot_general(
        a, b, (((0,), (0,)), ((), ())), precision=precision, preferred_element_type=F32
    )


def kernel(
    devices, cap,
    tracer_in, old_in, new_in, owner_in, local_in, coord_in, out,
    tracer, old_mass, new_mass, owner, local, coord, load,
    table, home_c, home_u, home_l, far_c, far_u, far_l, spread, la_home, la_far, fields,
    req_out, req_in, sum_out, sum_in, ans_out, ans_in, turned,
    req_send, req_recv, sum_send, sum_recv, ans_send, ans_recv,
):
    elems, levels, width = tracer.shape
    tracers = width // NODES
    points = levels * NODES
    cells = elems * levels
    group = points // cap
    blocks = devices // group
    me = lax.axis_index("elem")

    def peer(step):
        return lax.rem(me + step, devices)

    loads = [
        pltpu.make_async_copy(source, target, load.at[i])
        for i, (source, target) in enumerate(
            (
                (owner_in, owner),
                (local_in, local),
                (coord_in, coord),
                (new_in, new_mass),
                (old_in, old_mass),
                (tracer_in, tracer),
            )
        )
    ]
    for copy in loads:
        copy.start()

    barrier = pltpu.get_barrier_semaphore()

    @pl.loop(1, devices)
    def _(step):
        pl.semaphore_signal(barrier, inc=1, device_id=(peer(step),), device_id_type=MESH)

    for copy in loads[:4]:
        copy.wait()

    own = owner[...]
    away_ids = iota((devices, points), 0)
    away_ids = jnp.where(away_ids == me, -1, away_ids)
    hot = [(own[e : e + 1, :] == away_ids).astype(F32) for e in range(elems)]
    row, column = iota((points, 2 * points), 0), iota((points, 2 * points), 1)
    ladder = ((row <= column) | (column >= points)).astype(BF16)
    counted = jnp.dot(jnp.concatenate(hot, axis=0).astype(BF16), ladder, preferred_element_type=F32)
    before = jnp.zeros((devices, points), F32)
    base = (away_ids * cap).astype(F32)
    ranks, slots = [], []
    for e in range(elems):
        part = counted[e * devices : (e + 1) * devices]
        rank = jnp.sum(hot[e] * (part[:, :points] + before), axis=0, keepdims=True) - 1.0
        ranks.append(rank)
        slots.append(jnp.sum(hot[e] * base, axis=0, keepdims=True) + rank)
        before = before + part[:, points:]

    level_of = lax.div(iota((elems, points), 1), NODES)
    cell_home = (local[...] * levels + level_of).astype(F32)
    payload = [split3(x) for x in (cell_home, coord[0], coord[1], new_mass[...])]
    place = iota((cap, points), 0).astype(F32)
    chosen = []
    for term in range(3):
        lanes = []
        for e in range(elems):
            mine = place == ranks[e]
            lanes.append(
                jnp.concatenate(
                    [jnp.where(mine, f[term][e : e + 1, :], 0.0) for f in payload], axis=0
                ).astype(BF16)
            )
        chosen.append(jnp.concatenate(lanes, axis=1))
    hots = jnp.concatenate([h.astype(BF16) for h in hot], axis=1)
    asked = dot_nt(hots, chosen[0]) + dot_nt(hots, chosen[1]) + dot_nt(hots, chosen[2])
    req_out[...] = asked.reshape(devices, 1, points)
    req_in[pl.ds(me, 1)] = jnp.zeros((1, 1, points), F32)

    pl.semaphore_wait(barrier, devices - 1)

    def request(to, source):
        return pltpu.make_async_remote_copy(
            src_ref=req_out.at[to], dst_ref=req_in.at[source],
            send_sem=req_send.at[to], recv_sem=req_recv.at[source],
            device_id=(to,), device_id_type=MESH,
        )

    @pl.loop(1, devices)
    def _(step):
        request(peer(step), me).start()

    for copy in loads[4:]:
        copy.wait()

    flat = tracer[...].reshape(cells, width)
    table[...] = jnp.concatenate(split3(flat), axis=0).T.astype(BF16)

    point = iota((levels, points), 1)
    at_level = lax.div(point, NODES) == iota((levels, points), 0)
    masses = jnp.concatenate(
        [jnp.where(at_level, old_mass[e : e + 1, :], 0.0) for e in range(elems)], axis=0
    )
    widen = (
        lax.rem(iota((points, width), 0), NODES) == lax.div(iota((points, width), 1), tracers)
    ).astype(BF16)
    wide = jnp.zeros((cells, width), F32)
    for term in split3(masses):
        wide = wide + jnp.dot(term.astype(BF16), widen, preferred_element_type=F32)
    held = wide * flat
    by_node = held[:levels]
    for e in range(1, elems):
        by_node = by_node + held[e * levels : (e + 1) * levels]
    narrow = (lax.rem(iota((width, points), 0), tracers) == iota((width, points), 1)).astype(F32)
    source = jnp.dot(by_node, narrow, precision=HIGHEST, preferred_element_type=F32)

    cell_ids = lax.rem(iota((3 * cells, points), 0), cells).astype(F32)

    def evaluate(cell, wa, wb):
        chosen = (cell_ids == cell).astype(BF16)
        values = jnp.dot(table[...], chosen, preferred_element_type=F32)
        interp = lowest = highest = None
        for k in range(NODES):
            value = values[k * tracers : (k + 1) * tracers]
            term = (wa[k // 4] * wb[k % 4]) * value
            interp = term if k == 0 else interp + term
            lowest = value if k == 0 else jnp.minimum(lowest, value)
            highest = value if k == 0 else jnp.maximum(highest, value)
        clipped = jnp.minimum(jnp.maximum(interp, lowest), highest)
        margin = 0.01 + 0.05 * (highest - lowest)
        return clipped, highest + margin - clipped, clipped - lowest + margin

    def mass_sums(weights, clipped, upper, lower):
        rest = jnp.zeros((points - 3 * tracers, points), F32)
        terms = jnp.concatenate([-clipped, upper, lower, rest], axis=0)
        return dot_nt(weights, terms, HIGHEST)

    for i, value in enumerate(one_axis(coord[0]) + one_axis(coord[1])):
        la_home[i] = value.reshape(elems, 1, points)
    fields[pl.ds(0, elems)] = cell_home.reshape(elems, 1, points)
    fields[pl.ds(elems, elems)] = jnp.where(own == me, new_mass[...], 0.0).reshape(
        elems, 1, points
    )

    def home_block(e, sums):
        results = evaluate(
            fields[e], [la_home[i, e] for i in range(4)], [la_home[4 + i, e] for i in range(4)]
        )
        home_c[e], home_u[e], home_l[e] = results
        weights = jnp.where(at_level, fields[elems + e], 0.0)
        return sums + mass_sums(weights, *results)

    sums = lax.fori_loop(0, elems, home_block, source)

    slot_ids = iota((devices * cap, points), 0).astype(F32)
    for e in range(elems):
        spread[:, e * points : (e + 1) * points] = (slot_ids == slots[e]).astype(BF16)

    @pl.loop(1, devices)
    def _(step):
        request(peer(step), peer(step)).wait_recv()

    got = req_in[...].reshape(devices, points)
    r, c = iota((devices, points), 0), lax.div(iota((devices, points), 1), cap)
    bit = 1
    while bit < group:
        down = pltpu.roll(pltpu.roll(got, bit, 0), points - cap * bit, 1)
        up = pltpu.roll(pltpu.roll(got, devices - bit, 0), cap * bit, 1)
        row_bit, lane_bit = (r & bit) != 0, (c & bit) != 0
        got = jnp.where(row_bit == lane_bit, got, jnp.where(row_bit, down, up))
        bit *= 2
    la_far[4] = got.reshape(devices, 1, points)
    for i, value in enumerate(one_axis(got)):
        la_far[i] = value.reshape(devices, 1, points)

    level_ids = iota((levels, points), 0).astype(F32)

    def slot_level(b):
        cell = la_far[4, group * b]
        return cell, level_ids == cell - levels * jnp.floor((cell + 0.5) / levels)

    def far_block(b, sums):
        first = group * b
        cell, here = slot_level(b)
        results = evaluate(
            cell,
            [la_far[i, first + 1] for i in range(4)],
            [la_far[i, first + 2] for i in range(4)],
        )
        far_c[b], far_u[b], far_l[b] = results
        return sums + mass_sums(jnp.where(here, la_far[4, first + 3], 0.0), *results)

    sums = lax.fori_loop(0, blocks, far_block, sums)

    sum_out[...] = sums
    sum_in[pl.ds(me, 1)] = sums.reshape(1, levels, points)

    def share(to, source):
        return pltpu.make_async_remote_copy(
            src_ref=sum_out, dst_ref=sum_in.at[source],
            send_sem=sum_send.at[to], recv_sem=sum_recv.at[source],
            device_id=(to,), device_id_type=MESH,
        )

    @pl.loop(1, devices)
    def _(step):
        share(peer(step), me).start()

    @pl.loop(1, devices)
    def _(step):
        share(peer(step), peer(step)).wait_recv()

    total = jnp.sum(sum_in[...], axis=0)
    lane = iota((levels, points), 1)
    up_total = pltpu.roll(total, points - tracers, 1)
    down_total = pltpu.roll(total, points - 2 * tracers, 1)
    inside = lane < tracers
    plus = jnp.where(inside, jnp.maximum(total, 0.0) / jnp.where(inside, up_total, 1.0), 0.0)
    minus = jnp.where(inside, jnp.minimum(total, 0.0) / jnp.where(inside, down_total, 1.0), 0.0)
    factors = plus + pltpu.roll(minus, tracers, 1)

    def fix(here, clipped, upper, lower):
        by_lane = dot_tn(factors, here.astype(F32), HIGHEST)
        return clipped + by_lane[:tracers] * upper + by_lane[tracers : 2 * tracers] * lower

    def answer(to, source):
        return pltpu.make_async_remote_copy(
            src_ref=ans_out.at[to], dst_ref=ans_in.at[source],
            send_sem=ans_send.at[to], recv_sem=ans_recv.at[source],
            device_id=(to,), device_id_type=MESH,
        )

    lane_block = lax.div(iota((8, points), 1), cap)

    def swap_blocks(tiles):
        bit = 1
        while bit < group:
            moved = list(tiles)
            for t in range(group):
                if t & bit == 0:
                    odd = (lane_block & bit) != 0
                    a, b = tiles[t], tiles[t + bit]
                    moved[t] = jnp.where(odd, pltpu.roll(b, cap * bit, 1), a)
                    moved[t + bit] = jnp.where(odd, b, pltpu.roll(a, points - cap * bit, 1))
            tiles = moved
            bit *= 2
        return tiles

    my_place = lax.rem(me, group)

    def send_block(turn, carry):
        b = lax.rem(turn + lax.div(me, group), blocks)
        _, here = slot_level(b)
        fixed = fix(here, far_c[b], far_u[b], far_l[b])
        tiles = swap_blocks([fixed[8 * t : 8 * t + 8] for t in range(group)])
        last = fixed[8 * group :]
        for i in range(group):
            to = group * b + i
            ans_out[to, 0:8] = tiles[i]
            ans_out[to, 8:16] = pltpu.roll(last, lax.rem(my_place + group - i, group) * cap, 1)

            @pl.when(to != me)
            def _():
                answer(to, me).start()

        return carry

    lax.fori_loop(0, blocks, send_block, 0)

    def home_fix(e, carry):
        home_c[e] = fix(at_level, home_c[e], home_u[e], home_l[e])
        return carry

    lax.fori_loop(0, elems, home_fix, 0)
    ans_in[pl.ds(me, 1)] = jnp.zeros((1, 16, points), F32)

    @pl.loop(1, devices)
    def _(step):
        answer(peer(step), peer(step)).wait_recv()

    columns = []
    for b in range(blocks):
        tiles = swap_blocks([ans_in[group * b + i, 0:8] for i in range(group)])
        last = ans_in[group * b, 8:16]
        for i in range(1, group):
            last = jnp.where(lane_block == i, ans_in[group * b + i, 8:16], last)
        columns.append(jnp.concatenate(tiles + [last], axis=0))
    answers = jnp.concatenate(columns, axis=1)
    terms = jnp.concatenate(split3(answers), axis=0).astype(BF16)
    landed = jnp.dot(terms, spread[...], preferred_element_type=F32)
    landed = landed[:tracers] + landed[tracers : 2 * tracers] + landed[2 * tracers :]

    pad = jnp.zeros((points - tracers, points), F32)
    for e in range(elems):
        mixed = jnp.where(own[e : e + 1] == me, home_c[e], landed[:, e * points : (e + 1) * points])
        turned[e] = jnp.concatenate([mixed, pad], axis=0).T
        for k in range(NODES):
            out[e, :, k * tracers : (k + 1) * tracers] = turned[
                e, pl.ds(k, levels, stride=NODES), :
            ][:, :tracers]

    @pl.loop(1, devices)
    def _(step):
        to = peer(step)
        request(to, me).wait_send()
        share(to, me).wait_send()
        answer(to, me).wait_send()


def body(tracer, old_mass, new_mass, dep_owner, dep_local, dep_coord):
    devices = lax.axis_size("elem")
    elems, levels, width = tracer.shape
    tracers = width // NODES
    points = levels * NODES
    cap = elems * points // 32
    blocks = devices * cap // points
    cells = elems * levels
    vmem = pltpu.VMEM
    dma = pltpu.SemaphoreType.DMA
    return pl.pallas_call(
        functools.partial(kernel, devices, cap),
        out_shape=jax.ShapeDtypeStruct(tracer.shape, F32),
        in_specs=[pl.BlockSpec(memory_space=pltpu.HBM)] * 6,
        out_specs=pl.BlockSpec(memory_space=vmem),
        scratch_shapes=[
            vmem(tracer.shape, F32),
            vmem((elems, points), F32),
            vmem((elems, points), F32),
            vmem((elems, points), jnp.int32),
            vmem((elems, points), jnp.int32),
            vmem((2, elems, points), F32),
            dma((6,)),
            vmem((width, 3 * cells), BF16),
            *[vmem((elems, tracers, points), F32)] * 3,
            *[vmem((blocks, tracers, points), F32)] * 3,
            vmem((devices * cap, elems * points), BF16),
            vmem((8, elems, 1, points), F32),
            vmem((5, devices, 1, points), F32),
            vmem((2 * elems, 1, points), F32),
            vmem((devices, 1, points), F32),
            vmem((devices, 1, points), F32),
            vmem((levels, points), F32),
            vmem((devices, levels, points), F32),
            vmem((devices, 16, points), F32),
            vmem((devices, 16, points), F32),
            vmem((elems, points, points), F32),
            *[dma((devices,))] * 6,
        ],
        compiler_params=pltpu.CompilerParams(
            collective_id=0, has_side_effects=True, vmem_limit_bytes=64 * 1024 * 1024 - 65536
        ),
    )(
        tracer, old_mass, new_mass,
        dep_owner.reshape(elems, points), dep_local, dep_coord,
    )


def solution(mesh):
    placed = (
        P("elem", None, None),
        P("elem", None),
        P("elem", None),
        P("elem", None, None),
        P("elem", None),
        P(None, "elem", None),
    )
    return jax.shard_map(
        body, mesh=mesh, in_specs=placed, out_specs=P("elem", None, None), check_vma=False
    )
```

```python
import functools

import jax
import jax.numpy as jnp
from jax import lax
from jax.experimental import pallas as pl
from jax.experimental.pallas import tpu as pltpu
from jax.sharding import PartitionSpec as P

GLL_NODES = (-1.0, -0.4472135954999579, 0.4472135954999579, 1.0)
NODES = 16
MESH = pl.DeviceIdType.MESH
F32 = jnp.float32
BF16 = jnp.bfloat16
HIGHEST = lax.Precision.HIGHEST


def one_axis(coord):
    away = [coord - node for node in GLL_NODES]
    columns = []
    for own in range(4):
        factor, scale = None, 1.0
        for other in range(4):
            if other != own:
                factor = away[other] if factor is None else factor * away[other]
                scale *= GLL_NODES[own] - GLL_NODES[other]
        columns.append(factor * (1.0 / scale))
    return columns


def split3(x):
    high = x.astype(BF16).astype(F32)
    rest = x - high
    middle = rest.astype(BF16).astype(F32)
    return high, middle, rest - middle


def iota(shape, axis):
    return lax.broadcasted_iota(jnp.int32, shape, axis)


def dot_nt(a, b, precision=None):
    return lax.dot_general(
        a, b, (((1,), (1,)), ((), ())), precision=precision, preferred_element_type=F32
    )


def kernel(
    devices, cap,
    tracer_in, old_in, new_in, owner_in, local_in, coord_in, out,
    tracer, old_mass, new_mass, owner, local, coord, load,
    table, home_c, home_u, home_l, far_c, far_u, far_l, spread, la_home, la_far, fields,
    req_out, req_in, sum_out, sum_in, ans_out, ans_in, turned,
    req_send, req_recv, sum_send, sum_recv, ans_send, ans_recv,
):
    elems, levels, width = tracer.shape
    tracers = width // NODES
    points = levels * NODES
    cells = elems * levels
    group = points // cap
    blocks = devices // group
    me = lax.axis_index("elem")

    def peer(step):
        return lax.rem(me + step, devices)

    loads = [
        pltpu.make_async_copy(source, target, load.at[i])
        for i, (source, target) in enumerate(
            (
                (owner_in, owner),
                (local_in, local),
                (coord_in, coord),
                (new_in, new_mass),
                (old_in, old_mass),
                (tracer_in, tracer),
            )
        )
    ]
    for copy in loads:
        copy.start()

    barrier = pltpu.get_barrier_semaphore()

    @pl.loop(1, devices)
    def _(step):
        pl.semaphore_signal(barrier, inc=1, device_id=(peer(step),), device_id_type=MESH)

    for copy in loads[:4]:
        copy.wait()

    own = owner[...]
    away_ids = iota((devices, points), 0)
    away_ids = jnp.where(away_ids == me, -1, away_ids)
    hot = [(own[e : e + 1, :] == away_ids).astype(F32) for e in range(elems)]
    row, column = iota((points, 2 * points), 0), iota((points, 2 * points), 1)
    ladder = ((row <= column) | (column >= points)).astype(BF16)
    counted = jnp.dot(jnp.concatenate(hot, axis=0).astype(BF16), ladder, preferred_element_type=F32)
    before = jnp.zeros((devices, points), F32)
    base = (away_ids * cap).astype(F32)
    ranks, slots = [], []
    for e in range(elems):
        part = counted[e * devices : (e + 1) * devices]
        rank = jnp.sum(hot[e] * (part[:, :points] + before), axis=0, keepdims=True) - 1.0
        ranks.append(rank)
        slots.append(jnp.sum(hot[e] * base, axis=0, keepdims=True) + rank)
        before = before + part[:, points:]

    level_of = lax.div(iota((elems, points), 1), NODES)
    cell_home = (local[...] * levels + level_of).astype(F32)
    payload = [split3(x) for x in (cell_home, coord[0], coord[1], new_mass[...])]
    place = iota((cap, points), 0).astype(F32)
    chosen = []
    for term in range(3):
        lanes = []
        for e in range(elems):
            mine = place == ranks[e]
            lanes.append(
                jnp.concatenate(
                    [jnp.where(mine, f[term][e : e + 1, :], 0.0) for f in payload], axis=0
                ).astype(BF16)
            )
        chosen.append(jnp.concatenate(lanes, axis=1))
    hots = jnp.concatenate([h.astype(BF16) for h in hot], axis=1)
    asked = dot_nt(hots, chosen[0]) + dot_nt(hots, chosen[1]) + dot_nt(hots, chosen[2])
    req_out[...] = asked.reshape(devices, 1, points)
    req_in[pl.ds(me, 1)] = jnp.zeros((1, 1, points), F32)

    pl.semaphore_wait(barrier, devices - 1)

    def request(to, source):
        return pltpu.make_async_remote_copy(
            src_ref=req_out.at[to], dst_ref=req_in.at[source],
            send_sem=req_send.at[to], recv_sem=req_recv.at[source],
            device_id=(to,), device_id_type=MESH,
        )

    @pl.loop(1, devices)
    def _(step):
        request(peer(step), me).start()

    for copy in loads[4:]:
        copy.wait()

    flat = tracer[...].reshape(cells, width)
    table[...] = jnp.concatenate(split3(flat), axis=0).T.astype(BF16)

    point = iota((levels, points), 1)
    at_level = lax.div(point, NODES) == iota((levels, points), 0)
    masses = jnp.concatenate(
        [jnp.where(at_level, old_mass[e : e + 1, :], 0.0) for e in range(elems)], axis=0
    )
    widen = (
        lax.rem(iota((points, width), 0), NODES) == lax.div(iota((points, width), 1), tracers)
    ).astype(BF16)
    wide = jnp.zeros((cells, width), F32)
    for term in split3(masses):
        wide = wide + jnp.dot(term.astype(BF16), widen, preferred_element_type=F32)
    held = wide * flat
    by_node = held[:levels]
    for e in range(1, elems):
        by_node = by_node + held[e * levels : (e + 1) * levels]
    narrow = (lax.rem(iota((width, points), 0), tracers) == iota((width, points), 1)).astype(F32)
    source = jnp.dot(by_node, narrow, precision=HIGHEST, preferred_element_type=F32)

    cell_ids = lax.rem(iota((3 * cells, points), 0), cells).astype(F32)

    def evaluate(cell, wa, wb):
        chosen = (cell_ids == cell).astype(BF16)
        values = jnp.dot(table[...], chosen, preferred_element_type=F32)
        interp = lowest = highest = None
        for k in range(NODES):
            value = values[k * tracers : (k + 1) * tracers]
            term = (wa[k // 4] * wb[k % 4]) * value
            interp = term if k == 0 else interp + term
            lowest = value if k == 0 else jnp.minimum(lowest, value)
            highest = value if k == 0 else jnp.maximum(highest, value)
        clipped = jnp.minimum(jnp.maximum(interp, lowest), highest)
        margin = 0.01 + 0.05 * (highest - lowest)
        return clipped, highest + margin - clipped, clipped - lowest + margin

    def weighted(mass, clipped, upper, lower):
        rest = jnp.zeros((points - 3 * tracers, points), F32)
        return jnp.concatenate([-clipped * mass, upper * mass, lower * mass, rest], axis=0)

    def by_level(terms, here):
        parts = jnp.concatenate(split3(terms), axis=0).astype(BF16)
        found = dot_nt(parts, here.astype(F32).astype(BF16))
        return found[:points] + found[points : 2 * points] + found[2 * points :]

    for i, value in enumerate(one_axis(coord[0]) + one_axis(coord[1])):
        la_home[i] = value.reshape(elems, 1, points)
    fields[pl.ds(0, elems)] = cell_home.reshape(elems, 1, points)
    fields[pl.ds(elems, elems)] = jnp.where(own == me, new_mass[...], 0.0).reshape(
        elems, 1, points
    )

    def home_block(e, sums):
        results = evaluate(
            fields[e], [la_home[i, e] for i in range(4)], [la_home[4 + i, e] for i in range(4)]
        )
        home_c[e], home_u[e], home_l[e] = results
        return sums + weighted(fields[elems + e], *results)

    sums = lax.fori_loop(0, elems, home_block, jnp.zeros((points, points), F32), unroll=2)
    sums = by_level(sums, at_level)

    slot_ids = iota((devices * cap, points), 0).astype(F32)
    for e in range(elems):
        spread[:, e * points : (e + 1) * points] = (slot_ids == slots[e]).astype(BF16)

    @pl.loop(1, devices)
    def _(step):
        request(peer(step), peer(step)).wait_recv()

    got = req_in[...].reshape(devices, points)
    r, c = iota((devices, points), 0), lax.div(iota((devices, points), 1), cap)
    bit = 1
    while bit < group:
        down = pltpu.roll(pltpu.roll(got, bit, 0), points - cap * bit, 1)
        up = pltpu.roll(pltpu.roll(got, devices - bit, 0), cap * bit, 1)
        row_bit, lane_bit = (r & bit) != 0, (c & bit) != 0
        got = jnp.where(row_bit == lane_bit, got, jnp.where(row_bit, down, up))
        bit *= 2
    la_far[4] = got.reshape(devices, 1, points)
    for i, value in enumerate(one_axis(got)):
        la_far[i] = value.reshape(devices, 1, points)

    level_ids = iota((levels, points), 0).astype(F32)

    def slot_level(b):
        cell = la_far[4, group * b]
        return cell, level_ids == cell - levels * jnp.floor((cell + 0.5) / levels)

    def far_block(b, sums):
        first = group * b
        cell, here = slot_level(b)
        results = evaluate(
            cell,
            [la_far[i, first + 1] for i in range(4)],
            [la_far[i, first + 2] for i in range(4)],
        )
        far_c[b], far_u[b], far_l[b] = results
        return sums + by_level(weighted(la_far[4, first + 3], *results), here)

    sums = lax.fori_loop(0, blocks, far_block, sums, unroll=2)
    sums = source + sums.T

    sum_out[...] = sums
    sum_in[pl.ds(me, 1)] = sums.reshape(1, levels, points)

    def share(to, source):
        return pltpu.make_async_remote_copy(
            src_ref=sum_out, dst_ref=sum_in.at[source],
            send_sem=sum_send.at[to], recv_sem=sum_recv.at[source],
            device_id=(to,), device_id_type=MESH,
        )

    @pl.loop(1, devices)
    def _(step):
        share(peer(step), me).start()

    @pl.loop(1, devices)
    def _(step):
        share(peer(step), peer(step)).wait_recv()

    total = jnp.sum(sum_in[...], axis=0)
    lane = iota((levels, points), 1)
    up_total = pltpu.roll(total, points - tracers, 1)
    down_total = pltpu.roll(total, points - 2 * tracers, 1)
    inside = lane < tracers
    plus = jnp.where(inside, jnp.maximum(total, 0.0) / jnp.where(inside, up_total, 1.0), 0.0)
    minus = jnp.where(inside, jnp.minimum(total, 0.0) / jnp.where(inside, down_total, 1.0), 0.0)
    factors = plus + pltpu.roll(minus, tracers, 1)

    factors = jnp.concatenate(split3(factors), axis=0).T.astype(BF16)

    def spread_factors(here):
        thrice = jnp.concatenate([here.astype(F32)] * 3, axis=0).astype(BF16)
        return jnp.dot(factors, thrice, preferred_element_type=F32)

    def fix(by_lane, clipped, upper, lower):
        return clipped + by_lane[:tracers] * upper + by_lane[tracers : 2 * tracers] * lower

    def answer(to, source):
        return pltpu.make_async_remote_copy(
            src_ref=ans_out.at[to], dst_ref=ans_in.at[source],
            send_sem=ans_send.at[to], recv_sem=ans_recv.at[source],
            device_id=(to,), device_id_type=MESH,
        )

    lane_block = lax.div(iota((8, points), 1), cap)

    def swap_blocks(tiles):
        bit = 1
        while bit < group:
            moved = list(tiles)
            for t in range(group):
                if t & bit == 0:
                    odd = (lane_block & bit) != 0
                    a, b = tiles[t], tiles[t + bit]
                    moved[t] = jnp.where(odd, pltpu.roll(b, cap * bit, 1), a)
                    moved[t + bit] = jnp.where(odd, b, pltpu.roll(a, points - cap * bit, 1))
            tiles = moved
            bit *= 2
        return tiles

    my_place = lax.rem(me, group)

    def send_block(turn, carry):
        b = lax.rem(turn + lax.div(me, group), blocks)
        _, here = slot_level(b)
        fixed = fix(spread_factors(here), far_c[b], far_u[b], far_l[b])
        tiles = swap_blocks([fixed[8 * t : 8 * t + 8] for t in range(group)])
        last = fixed[8 * group :]
        for i in range(group):
            to = group * b + i
            ans_out[to, 0:8] = tiles[i]
            ans_out[to, 8:16] = pltpu.roll(last, lax.rem(my_place + group - i, group) * cap, 1)

            @pl.when(to != me)
            def _():
                answer(to, me).start()

        return carry

    lax.fori_loop(0, blocks, send_block, 0, unroll=2)

    home_factors = spread_factors(at_level)

    def home_fix(e, carry):
        home_c[e] = fix(home_factors, home_c[e], home_u[e], home_l[e])
        return carry

    lax.fori_loop(0, elems, home_fix, 0, unroll=2)
    ans_in[pl.ds(me, 1)] = jnp.zeros((1, 16, points), F32)

    @pl.loop(1, devices)
    def _(step):
        answer(peer(step), peer(step)).wait_recv()

    columns = []
    for b in range(blocks):
        tiles = swap_blocks([ans_in[group * b + i, 0:8] for i in range(group)])
        last = ans_in[group * b, 8:16]
        for i in range(1, group):
            last = jnp.where(lane_block == i, ans_in[group * b + i, 8:16], last)
        columns.append(jnp.concatenate(tiles + [last], axis=0))
    answers = jnp.concatenate(columns, axis=1)
    terms = jnp.concatenate(split3(answers), axis=0).astype(BF16)
    landed = jnp.dot(terms, spread[...], preferred_element_type=F32)
    landed = landed[:tracers] + landed[tracers : 2 * tracers] + landed[2 * tracers :]

    pad = jnp.zeros((points - tracers, points), F32)
    for e in range(elems):
        mixed = jnp.where(own[e : e + 1] == me, home_c[e], landed[:, e * points : (e + 1) * points])
        turned[e] = jnp.concatenate([mixed, pad], axis=0).T
        for k in range(NODES):
            out[e, :, k * tracers : (k + 1) * tracers] = turned[
                e, pl.ds(k, levels, stride=NODES), :
            ][:, :tracers]

    @pl.loop(1, devices)
    def _(step):
        to = peer(step)
        request(to, me).wait_send()
        share(to, me).wait_send()
        answer(to, me).wait_send()


def body(tracer, old_mass, new_mass, dep_owner, dep_local, dep_coord):
    devices = lax.axis_size("elem")
    elems, levels, width = tracer.shape
    tracers = width // NODES
    points = levels * NODES
    cap = elems * points // 32
    blocks = devices * cap // points
    cells = elems * levels
    vmem = pltpu.VMEM
    dma = pltpu.SemaphoreType.DMA
    return pl.pallas_call(
        functools.partial(kernel, devices, cap),
        out_shape=jax.ShapeDtypeStruct(tracer.shape, F32),
        in_specs=[pl.BlockSpec(memory_space=pltpu.HBM)] * 6,
        out_specs=pl.BlockSpec(memory_space=vmem),
        scratch_shapes=[
            vmem(tracer.shape, F32),
            vmem((elems, points), F32),
            vmem((elems, points), F32),
            vmem((elems, points), jnp.int32),
            vmem((elems, points), jnp.int32),
            vmem((2, elems, points), F32),
            dma((6,)),
            vmem((width, 3 * cells), BF16),
            *[vmem((elems, tracers, points), F32)] * 3,
            *[vmem((blocks, tracers, points), F32)] * 3,
            vmem((devices * cap, elems * points), BF16),
            vmem((8, elems, 1, points), F32),
            vmem((5, devices, 1, points), F32),
            vmem((2 * elems, 1, points), F32),
            vmem((devices, 1, points), F32),
            vmem((devices, 1, points), F32),
            vmem((levels, points), F32),
            vmem((devices, levels, points), F32),
            vmem((devices, 16, points), F32),
            vmem((devices, 16, points), F32),
            vmem((elems, points, points), F32),
            *[dma((devices,))] * 6,
        ],
        compiler_params=pltpu.CompilerParams(
            collective_id=0, has_side_effects=True, vmem_limit_bytes=64 * 1024 * 1024 - 65536
        ),
    )(
        tracer, old_mass, new_mass,
        dep_owner.reshape(elems, points), dep_local, dep_coord,
    )


def solution(mesh):
    placed = (
        P("elem", None, None),
        P("elem", None),
        P("elem", None),
        P("elem", None, None),
        P("elem", None),
        P(None, "elem", None),
    )
    return jax.shard_map(
        body, mesh=mesh, in_specs=placed, out_specs=P("elem", None, None), check_vma=False
    )
```
